256 devices in a mesh: dom: 64 (over y, z, core), sub: 4 (over x).
Axes of the slice: x: 4, y: 4, z: 8, core: 2. Of those that a mesh axis runs over, the one named last changes fastest.
Arguments:
- a_blocks: bfloat16 [4096, 64, 448], P(('dom', 'sub')), may hold values from -0.25 to 0.25
- a_nbrs: int32 [4096, 6], P(('dom', 'sub')), may hold values from 0 to 143
- p_blocks: bfloat16 [4096, 64, 128], P(('dom', 'sub')), may hold values from -3 to 3
- p_dest: int32 [4096, 1], P(('dom', 'sub')), may hold values from 0 to 63; in each aligned block of 16 rows (0 to 15, 16 to 31, ...) at most 2 rows name the same one
- p_far_agg: int32 [4096, 1], P(('dom', 'sub')), may hold values from 0 to 1
- agg_id: int32 [256, 16], P(('dom', 'sub')), may hold values from 0 to 1, never falling along the last dimension, each value on 1 to 15 neighbouring positions
- ap_slot: int32 [4096, 7, 2], P(('dom', 'sub')), may hold values from 0 to 7
- c_slot: int32 [4096, 2, 8], P(('dom', 'sub')), may hold values from 0 to 5
- send_rows: int32 [16384, 2], P(('dom', 'sub')), may hold values from 0 to 15
Outputs:
- coarse: bfloat16 [512, 64, 384], P('dom')
The draws below stay inside these ranges and needn't reach their ends.
Inputs may be any that keep to these rules, and one draw needn't show every extreme that they name: `a_nbrs`: entries below 16 are rows of the same device; entry 16 + p * 2 + f is the f-th row sent by device p of the same sub index. `p_dest`: among one device's 16 rows no dom index is named by more than 2 rows, and some device's rows reach that bound. `agg_id`: never falling along a device's rows; each aggregate holds 1 to 15 rows.
All inputs are finite; a program needn't handle non-finite values.
Results may differ from the reference program's by a relative error of at most 0.005.
Values may be sent and summed in bfloat16 or wider, within the bound.
A program may use at most 192 MiB of HBM per device.

```python
import math
import jax
import jax.numpy as jnp
import numpy as np
from jax import lax

B = 64
CB = 64
KA = 7
KP = 2
KAP = 8
KC = 6
R = 16
AGG_DEV = 2
AGG_MOST = 15
FETCH_SLOTS = 2
RET_SLOTS = 2
DEVS = 256
ROWS = 4096
CROWS = 512
N_DOM = 64
N_SUB = 4


def with_ends(array, stream_key, smallest, high):
    longest = array.shape.index(max(array.shape))
    spots = []
    for shift in (0, 1):
        where = [jax.random.randint(jax.random.fold_in(stream_key, axis), (), 0, length) for axis, length in enumerate(array.shape)]
        where[longest] = (where[longest] + shift) % array.shape[longest]
        spots.append(tuple(where))
    return array.at[spots[0]].set(smallest).at[spots[1]].set(high)


def block_levels(stream_key, dims, cuts, low, top_value):
    loudness = 1.0
    for dim, shards_of in cuts:
        heights = jax.random.uniform(jax.random.fold_in(jax.random.fold_in(stream_key, 6), dim), (shards_of,), jnp.float32, low / len(cuts), top_value / len(cuts))
        loudness = loudness * jnp.repeat(jnp.exp(heights), dims[dim] // shards_of).reshape((-1,) + (1,) * (len(dims) - 1 - dim))
    return loudness


def split_up(number_of, total, limit, skew):
    portions = [(1 << 20) // math.isqrt(grade ** skew) + 1 for grade in range(2, number_of + 1)]
    rest, given = total - limit - (number_of - 1), [1] * (number_of - 1)
    while rest > 0:
        free = [i for i in range(number_of - 1) if given[i] < limit]
        pool, remaining = sum([portions[i] for i in free]), rest
        for i in free:
            addition = min(limit - given[i], max(1, remaining * portions[i] // pool), rest)
            given[i] = given[i] + addition
            rest = rest - addition
    return np.array([limit] + given)


def uneven_parts(key, amount, total, reach, slope):
    if amount == 2:
        one = jax.random.randint(key, (), max(1, total - reach), min(reach, total - 1) + 1)
        return jnp.stack([one, total - one])
    sizes = jnp.asarray(split_up(amount, total, reach, slope), jnp.int32)
    couples = (amount - 1) // 2
    source_of, taker = sizes[1:1 + 2 * couples:2], sizes[2:2 + 2 * couples:2]
    margin = jnp.minimum(source_of - 1, reach - taker)
    passed = jax.random.randint(jax.random.fold_in(key, 1), (couples,), 0, 1 << 20) % (margin + 1)
    sizes = sizes.at[1:1 + 2 * couples:2].set(source_of - passed).at[2:2 + 2 * couples:2].set(taker + passed)
    return sizes[jax.random.permutation(jax.random.fold_in(key, 2), amount)]


def assign_block(stream_key, own, number, rows, number_of, top, limit, slope):
    ranking = jax.random.permutation(stream_key, number_of)
    crowded, common = portions_of(number_of, rows * top, limit, slope, True), portions_of(number_of, rows * top, limit, slope, False)
    places = jnp.arange(number_of)

    def named(lengths, rotation):
        used = int((lengths > 0).sum())
        fixed = max(1, used // 4)
        passed = fixed + (places - fixed + rotation * (used - fixed)) % max(1, number_of - fixed)
        return jnp.zeros((number_of,), jnp.int32).at[ranking[jnp.where(places < fixed, places, passed)]].set(jnp.asarray(lengths, jnp.int32))

    lengths = jnp.where(number % 4 == 0, named(crowded, number // 4), named(common, number - number // 4 - 1))
    mixed = jax.random.permutation(jax.random.fold_in(own, 3), number_of)
    giver, taker = mixed[0:number_of // 2 * 2:2], mixed[1:number_of // 2 * 2:2]
    room = jnp.minimum(lengths[giver] - 1, limit - lengths[taker]) // 2
    room = jnp.where((giver == ranking[0]) | (taker == ranking[0]) | (lengths[taker] == 0), 0, jnp.maximum(room, 0))
    passed = jax.random.randint(jax.random.fold_in(own, 4), (number_of // 2,), 0, 1 << 20) % (room + 1)
    lengths = lengths.at[giver].add(-passed).at[taker].add(passed)
    members = jnp.searchsorted(jnp.cumsum(lengths), jnp.arange(rows * top), side="right").astype(jnp.int32)
    grid = members.reshape(top, rows).T
    grid = grid[jax.random.permutation(jax.random.fold_in(own, 1), rows)]
    rotation = jax.random.randint(jax.random.fold_in(own, 2), (rows, 1), 0, top)
    return jnp.take_along_axis(grid, (jnp.arange(top)[None, :] + rotation) % top, axis=1)


def portions_of(count, total, limit, slope, full):
    portions = [(1 << 20) // math.isqrt(grade ** slope) + 1 for grade in range(1, count + 1)]
    largest = limit if full else min(limit, max(-(-total // count), total * portions[0] // sum(portions)))
    least = 1 if total - largest >= count - 1 else 0
    counts, spare = [largest] + [least] * (count - 1), total - largest - least * (count - 1)
    while spare > 0:
        movable = [i for i in range(1, count) if counts[i] < largest] or [i for i in range(1, count) if counts[i] < limit]
        whole, left = sum([portions[i] for i in movable]), spare
        for i in movable:
            more = min(limit - counts[i], max(1, left * portions[i] // whole), spare)
            counts[i] = counts[i] + more
            spare = spare - more
    return np.array(counts)


def normal_values(stream_key, extent, scale, reach, split=(), dtype=jnp.bfloat16):
    loudness = block_levels(stream_key, extent, split, -0.22, 0.18) if split else 1.0
    array = jax.random.normal(stream_key, extent, jnp.float32) * scale * loudness
    return jnp.minimum(jnp.maximum(array, -reach), reach).astype(dtype)


def setup_inputs(seed: int = 0) -> dict:
    key_list = jax.random.split(jax.random.key(seed), 10)
    a_blocks = normal_values(key_list[0], (ROWS, B, KA * B), (KA * B) ** -0.5, 0.25, ((0, 256),))
    a_nbrs = with_ends(jax.random.randint(key_list[1], (ROWS, KA - 1), 0, R + N_DOM * FETCH_SLOTS), jax.random.fold_in(key_list[1], 1), 0, (R + N_DOM * FETCH_SLOTS) - 1).astype(jnp.int32)
    p_blocks = normal_values(key_list[2], (ROWS, B, KP * CB), 0.5, 3.0, ((0, 256),))
    p_dest_keys = jax.random.split(jax.random.fold_in(key_list[3], 1), ROWS // R)
    p_dest_turns = jax.random.permutation(jax.random.fold_in(key_list[3], 3), ROWS // R)
    p_dest = jax.vmap(lambda own, number: assign_block(jax.random.fold_in(key_list[3], 2), own, number, R, N_DOM, 1, RET_SLOTS, 2))(p_dest_keys, p_dest_turns).reshape((ROWS, 1))
    p_far_agg = with_ends(jax.random.randint(key_list[4], (ROWS, 1), 0, AGG_DEV), jax.random.fold_in(key_list[4], 1), 0, AGG_DEV - 1).astype(jnp.int32)
    agg_id = jax.vmap(lambda own: jnp.searchsorted(jnp.cumsum(uneven_parts(own, AGG_DEV, R, AGG_MOST, 1)), jnp.arange(R), side="right"))(jax.random.split(key_list[5], DEVS)).reshape((DEVS, R)).astype(jnp.int32)
    ap_slot = with_ends(jax.random.randint(key_list[6], (ROWS, KA, KP), 0, KAP), jax.random.fold_in(key_list[6], 1), 0, KAP - 1).astype(jnp.int32)
    c_slot = with_ends(jax.random.randint(key_list[7], (ROWS, KP, KAP), 0, KC), jax.random.fold_in(key_list[7], 1), 0, KC - 1).astype(jnp.int32)
    send_rows = with_ends(jax.random.randint(key_list[8], (DEVS * N_DOM, FETCH_SLOTS), 0, R), jax.random.fold_in(key_list[8], 1), 0, R - 1).astype(jnp.int32)
    return dict(a_blocks=a_blocks, a_nbrs=a_nbrs, p_blocks=p_blocks, p_dest=p_dest, p_far_agg=p_far_agg, agg_id=agg_id, ap_slot=ap_slot, c_slot=c_slot, send_rows=send_rows)


def place_blocks(coarse_sum, contrib, targets):
    item_count = contrib.shape[0]
    coarse_width = contrib.shape[1]
    blocks = contrib.reshape(item_count, coarse_width, -1, coarse_width).transpose(0, 2, 1, 3)
    blocks = blocks.reshape(-1, coarse_width, coarse_width)
    return coarse_sum.at[targets.reshape(-1)].add(blocks, mode="drop")


def reference(a_blocks, a_nbrs, p_blocks, p_dest, p_far_agg, agg_id, ap_slot, c_slot, send_rows):
    send_three = send_rows.reshape(DEVS, N_DOM, FETCH_SLOTS)
    local_iota = jnp.arange(R).astype(jnp.int32)
    peer_iota = jnp.arange(N_DOM).astype(jnp.int32)
    merge_iota = jnp.arange(KAP).astype(jnp.int32)
    highest = lax.Precision.HIGHEST

    def device_step(coarse_sum, device):
        dom_index = device // N_SUB
        sub_index = device % N_SUB
        senders = (peer_iota * N_SUB + sub_index).astype(jnp.int32)
        received = send_three[senders, dom_index, :]
        remote_rows = (senders[:, None] * R + received).reshape(-1)
        ext_rows = jnp.concatenate([device * R + local_iota, remote_rows]).astype(jnp.int32)
        row_start = (device * R).astype(jnp.int32)
        a_dev = lax.dynamic_slice_in_dim(a_blocks, row_start, R, 0).astype(jnp.float32)
        nbrs_dev = lax.dynamic_slice_in_dim(a_nbrs, row_start, R, 0)
        p_dev = lax.dynamic_slice_in_dim(p_blocks, row_start, R, 0).astype(jnp.float32)
        dest_dev = lax.dynamic_slice_in_dim(p_dest, row_start, R, 0)
        far_dev = lax.dynamic_slice_in_dim(p_far_agg, row_start, R, 0)
        slot_dev = lax.dynamic_slice_in_dim(ap_slot, row_start, R, 0)
        cslot_dev = lax.dynamic_slice_in_dim(c_slot, row_start, R, 0)
        agg_dev = agg_id[device]
        columns = jnp.concatenate([local_iota[:, None], nbrs_dev], axis=1)
        gathered = p_blocks[ext_rows[columns]].astype(jnp.float32)
        product = jnp.einsum("rbke,rkec->rkbc", a_dev.reshape(R, B, KA, B), gathered, precision=highest)
        select = (slot_dev[..., None] == merge_iota).astype(jnp.float32)
        merged = jnp.einsum("rkblc,rklq->rbqc", product.reshape(R, KA, B, KP, CB), select, precision=highest)
        merged = merged.reshape(R, B, KAP * CB).astype(jnp.bfloat16)
        contrib = jnp.einsum("rbmc,rbx->rmcx", p_dev.reshape(R, B, KP, CB), merged.astype(jnp.float32), precision=highest)
        near_slots = (device * AGG_DEV + agg_dev)[:, None] * KC + cslot_dev[:, 0, :]
        far_row = (dest_dev[:, 0] * N_SUB + sub_index) * AGG_DEV + far_dev[:, 0]
        far_slots = far_row[:, None] * KC + cslot_dev[:, 1, :]
        coarse_sum = place_blocks(coarse_sum, contrib[:, 0], near_slots.astype(jnp.int32))
        coarse_sum = place_blocks(coarse_sum, contrib[:, 1], far_slots.astype(jnp.int32))
        return coarse_sum, None

    coarse_sum = jnp.zeros((CROWS * KC, CB, CB), jnp.float32)
    coarse_sum, unused = lax.scan(device_step, coarse_sum, jnp.arange(DEVS).astype(jnp.int32))
    coarse = coarse_sum.reshape(CROWS, KC, CB, CB).transpose(0, 2, 1, 3).reshape(CROWS, CB, KC * CB)
    return coarse.astype(jnp.bfloat16)
```

```python
import functools

import jax
import jax.numpy as jnp
from jax import lax
from jax.experimental import pallas as pl
from jax.experimental.pallas import tpu as pltpu
from jax.sharding import PartitionSpec as P

MESH = pl.DeviceIdType.MESH
NZ = 8
NC = 2
R = 16
KA = 7
B = 64
AGG = 2
KC = 6
CHUNK = 8
f32, bf16, i32 = jnp.float32, jnp.bfloat16, jnp.int32


def kernel(ny, nx, nbr_s, dest_s, far_s, agg_s, slot_s, cslot_s, send_s, a_hbm, p_ref, out_ref, *scr):
    nz, nc = NZ, NC
    half = nz // 2
    nyc = ny * nc
    ml = B // nyc
    tr = nyc * AGG
    sl = ml * R
    near_rows = ml * AGG
    scr = list(scr)
    zr = [scr.pop(0) for _ in range(half - 1)]
    zl = [scr.pop(0) for _ in range(half - 1)]
    (zfar, a_vm, idx_out, idx_in, idx_s, cols_s, picks, ext, wbuf, near, wsend, r1, meta_out, meta_in, zsend, r2, total, osend, r3,
     a_sem, s_ring, r_ring, s_idx, r_idx, l_idx, s_pick, r_pick, s_one, r_one, s_meta, r_meta, s_two, r_two, s_three, r_three) = scr

    dom, x = lax.axis_index("dom"), lax.axis_index("sub")
    y = lax.div(dom, nz * nc)
    z = lax.rem(lax.div(dom, nc), nz)
    c = lax.rem(dom, nc)
    j = y * nc + c

    def along_z(step):
        return ((y * nz + lax.rem(z + step + nz, nz)) * nc + c, x)

    def in_plane(peer, px):
        return ((lax.div(peer, nc) * nz + z) * nc + lax.rem(peer, nc), px)

    def remote(src, dst, send, recv, device):
        return pltpu.make_async_remote_copy(
            src_ref=src, dst_ref=dst, send_sem=send, recv_sem=recv, device_id=device, device_id_type=MESH
        )

    def loop(lo, hi, fn):
        lax.fori_loop(lo, hi, lambda t, carry: (fn(t), carry)[1], 0)

    a_copy = pltpu.make_async_copy(a_hbm, a_vm, a_sem)
    a_copy.start()

    barrier = pltpu.get_barrier_semaphore()
    group = nx * nyc
    place = x * nyc + j
    loop(1, nz, lambda t: pl.semaphore_signal(barrier, inc=1, device_id=along_z(t), device_id_type=MESH))

    def greet(t):
        q = lax.rem(place + t, group)
        pl.semaphore_signal(barrier, inc=1, device_id=in_plane(lax.rem(q, nyc), lax.div(q, nyc)), device_id_type=MESH)

    loop(1, group, greet)
    pl.semaphore_wait(barrier, nz - 1 + group - 1)

    def ring(way, step, piece):
        there = (zr, zl)[way]
        src = p_ref if step == 1 else there[step - 2]
        dst = there[step - 1] if step < half else zfar
        rows = pl.ds(piece * CHUNK, CHUNK)
        return remote(
            src.at[rows], dst.at[rows], s_ring.at[way, step - 1, piece], r_ring.at[way, step - 1, piece],
            along_z(1 if way == 0 else -1),
        )

    pieces = R // CHUNK

    def order(way, step):
        listed = list(range(pieces)) if way == 0 else list(range(pieces))[::-1]
        return listed if step < half else listed[: pieces // 2]

    for piece in range(pieces):
        for way in (0, 1):
            ring(way, 1, order(way, 1)[piece]).start()

    lane = lax.broadcasted_iota(i32, (8, 128), 1)

    def list_for(t):
        zt = lax.rem(z + t, nz)
        tile = jnp.zeros((8, 128), i32)
        for peer in range(nyc):
            for f in range(2):
                row = send_s[((peer // nc) * nz + zt) * nc + peer % nc, f]
                tile = jnp.where(lane == peer * 2 + f, row, tile)
        return tile

    def slot_of(t):
        return 0 if t == 0 else 2 * t - 1 if t < half else nz - 1 if t == half else 2 * (nz - t)

    idx_in[0] = list_for(0)
    index_copies = []
    for t in range(1, nz):
        idx_out[t] = list_for(t)
        copy = remote(idx_out.at[t], idx_in.at[slot_of(t)], s_idx.at[t], r_idx.at[t], along_z(t))
        copy.start()
        index_copies.append(copy)

    def message(number):
        first = 0 if number == 0 else 2 * number - 1
        return first, (1 if number in (0, half) else 2)

    def pick_copy(number, t):
        first, count = message(number)
        return remote(
            picks.at[t, pl.ds(first * 2, count * 2)], ext.at[pl.ds(R + (j * nz + first) * 2, count * 2)],
            s_pick.at[number, t], r_pick.at[number, t], in_plane(lax.rem(j + t, nyc), x),
        )

    def pick(number, sources, index):
        first, count = message(number)
        for n, source in enumerate(sources):
            for f in range(2):
                ext[R + (j * nz + first + n) * 2 + f] = source[index(first + n, j, f)]

        def for_peer(t):
            peer = lax.rem(j + t, nyc)
            for n, source in enumerate(sources):
                for f in range(2):
                    picks[t, (first + n) * 2 + f] = source[index(first + n, peer, f)]
            pick_copy(number, t).start()

        loop(1, nyc, for_peer)

    pick(0, [p_ref], lambda slot, peer, f: send_s[(lax.div(peer, nc) * nz + z) * nc + lax.rem(peer, nc), f])
    ext[0:R] = p_ref[...]

    def place_row(i):
        cols_s[i * KA] = i
        for k in range(1, KA):
            n = nbr_s[i, k - 1]
            e = n - R
            f = e & 1
            owner = e >> 1
            oc = owner & (nc - 1)
            oz = (owner >> (nc.bit_length() - 1)) & (nz - 1)
            oy = owner >> ((nz * nc).bit_length() - 1)
            dz = (oz - z + nz) & (nz - 1)
            slot = jnp.where(dz == half, nz - 1, jnp.where(dz < half, 2 * dz, 2 * (nz - dz) - 1))
            cols_s[i * KA + k] = jnp.where(n < R, n, R + ((oy * nc + oc) * nz + slot) * 2 + f)

    loop(0, R, place_row)

    for copy in index_copies:
        copy.wait()
    to_scalars = pltpu.make_async_copy(idx_in, idx_s, l_idx)
    to_scalars.start()
    to_scalars.wait()
    listed = lambda slot, peer, f: idx_s[slot, 0, peer * 2 + f]

    for step in range(1, half + 1):
        for n in range(len(order(0, step))):
            for way in (0, 1):
                piece = order(way, step)[n]
                ring(way, step, piece).wait_recv()
                if step < half and piece in order(way, step + 1):
                    ring(way, step + 1, piece).start()
        pick(step, [zr[step - 1], zl[step - 1]] if step < half else [zfar], listed)
    for number in range(half + 1):
        loop(1, nyc, lambda t, number=number: pick_copy(number, t).wait_recv())
    a_copy.wait()

    lane1 = lax.broadcasted_iota(i32, (1, 128), 1)
    low = lane1 < B
    high = jnp.where(low, 0, 1)
    low_mask = jnp.where(low, 1.0, 0.0).astype(bf16)
    high_mask = jnp.where(low, 0.0, 1.0).astype(bf16)
    near[...] = jnp.zeros_like(near)

    def masks(s0, s1, pairs):
        same = jnp.where(low, s0, s1) - high
        cross = jnp.where(low, s1, s0) - high
        return [
            (jnp.where(same == 2 * q, 1.0, 0.0).astype(f32), jnp.where(cross == 2 * q, 1.0, 0.0).astype(f32))
            for q in range(pairs)
        ]

    def row(i):
        ap = [None] * 4

        def merge(k, q):
            turned = pltpu.roll(q, B, 1)
            for n, (same, cross) in enumerate(masks(slot_s[i, k, 0], slot_s[i, k, 1], 4)):
                term = q * same + turned * cross
                ap[n] = term if ap[n] is None else ap[n] + term

        for pair in range(KA // 2):
            a = a_vm[i, :, pair * 128:(pair + 1) * 128]
            left = jnp.concatenate([a * low_mask, a * high_mask], axis=0)
            right = jnp.concatenate([ext[cols_s[i * KA + 2 * pair]], ext[cols_s[i * KA + 2 * pair + 1]]], axis=0)
            q = jnp.dot(left, right, preferred_element_type=f32)
            merge(2 * pair, q[:B])
            merge(2 * pair + 1, q[B:])
        q = jnp.dot(a_vm[i, :, (KA - 1) * B:], ext[cols_s[i * KA + KA - 1]], preferred_element_type=f32)
        merge(KA - 1, q)
        merged = jnp.concatenate([block.astype(bf16) for block in ap], axis=1)
        w = lax.dot_general(p_ref[i], merged, (((0,), (0,)), ((), ())), preferred_element_type=f32)
        near_to, far_to = [None] * 3, [None] * 3
        for q in range(4):
            block = w[:, q * 128:(q + 1) * 128]
            turned = pltpu.roll(block, B, 1)
            for m, to in ((0, near_to), (1, far_to)):
                lines = slice(m * B, (m + 1) * B)
                for n, (same, cross) in enumerate(masks(cslot_s[i, m, 2 * q], cslot_s[i, m, 2 * q + 1], 3)):
                    term = block[lines] * same + turned[lines] * cross
                    to[n] = term if to[n] is None else to[n] + term
        agg = agg_s[0, i]
        for n in range(3):
            wbuf[n, pl.ds(i, B, stride=R), :] = far_to[n]
            for g in range(AGG):
                near[g, :, n * 128:(n + 1) * 128] += near_to[n] * jnp.where(agg == g, 1.0, 0.0).astype(f32)

    loop(0, R, row)

    meta = jnp.zeros((8, 128), i32)
    for i in range(R):
        d = dest_s[i, 0]
        dc = d & (nc - 1)
        dz = (d >> (nc.bit_length() - 1)) & (nz - 1)
        dy = d >> ((nz * nc).bit_length() - 1)
        meta = jnp.where(lane == j * R + i, dz * tr + (dy * nc + dc) * AGG + far_s[i, 0], meta)
    meta_out[...] = meta

    def share(peer):
        for n in range(3):
            wsend[peer, 0:sl, n * 128:(n + 1) * 128] = wbuf[n, pl.ds(peer * sl, sl), :].astype(bf16)
        lines = jnp.concatenate([near[g, pl.ds(peer * ml, ml), :] for g in range(AGG)], axis=0)
        wsend[peer, sl:sl + near_rows, :] = lines.astype(bf16)

    def one(t):
        peer = lax.rem(j + t, nyc)
        return remote(wsend.at[peer], r1.at[j], s_one.at[t], r_one.at[t], in_plane(peer, x))

    def tell(t):
        return remote(meta_out, meta_in.at[j], s_meta.at[t], r_meta.at[t], in_plane(lax.rem(j + t, nyc), x))

    def send_one(t):
        tell(t).start()
        share(lax.rem(j + t, nyc))
        one(t).start()

    loop(1, nyc, send_one)
    share(j)
    r1[j] = wsend[j]
    meta_in[j] = meta_out[...]

    def wait_one(t):
        tell(t).wait_recv()
        one(t).wait_recv()

    loop(1, nyc, wait_one)

    told = meta_in[0]
    for peer in range(1, nyc):
        told = told + meta_in[peer]
    width = nyc * R
    aimed = lax.broadcasted_iota(i32, (nz * tr, width), 0) == told[0:1, 0:width]
    aimed = jnp.where(aimed, 1.0, 0.0).astype(bf16)
    for m in range(ml):
        lines = jnp.concatenate([r1[peer, m * R:(m + 1) * R, :] for peer in range(nyc)], axis=0)
        summed = jnp.dot(aimed, lines, preferred_element_type=f32).astype(bf16)
        for zt in range(nz):
            zsend[zt, m * tr:(m + 1) * tr, :] = summed[zt * tr:(zt + 1) * tr]

    def two(t):
        return remote(zsend.at[lax.rem(z + t, nz)], r2.at[t], s_two.at[t], r_two.at[t], along_z(t))

    for t in [half] + [t for s in range(half - 1, 0, -1) for t in (s, nz - s)]:
        two(t).start()
    sums = zsend[z].astype(f32)
    for t in [t for s in range(1, half) for t in (s, nz - s)] + [half]:
        two(t).wait_recv()
        sums = sums + r2[t].astype(f32)
    for n in range(3):
        total[n] = sums[:, n * 128:(n + 1) * 128]

    for peer in range(nyc):
        lines = [
            jnp.concatenate([total[n, pl.ds(peer * AGG + g, ml, stride=tr), :] for g in range(AGG)], axis=0)
            for n in range(3)
        ]
        lines = jnp.concatenate(lines, axis=1) + r1[peer, sl:sl + near_rows, :].astype(f32)
        osend[peer] = lines.astype(bf16)

    def three(t):
        q = lax.rem(place + t, group)
        peer = lax.rem(q, nyc)
        return remote(osend.at[peer], r3.at[place], s_three.at[t], r_three.at[t], in_plane(peer, lax.div(q, nyc)))

    loop(1, group, lambda t: three(t).start())
    r3[place] = osend[j]
    loop(1, group, lambda t: three(t).wait_recv())
    for px in range(nx):
        for g in range(AGG):
            lines = [r3[px * nyc + peer].astype(f32)[g * ml:(g + 1) * ml] for peer in range(nyc)]
            out_ref[px * AGG + g] = jnp.concatenate(lines, axis=0).astype(bf16)

    for way in (0, 1):
        for step in range(1, half + 1):
            for piece in order(way, step):
                ring(way, step, piece).wait_send()
    for number in range(half + 1):
        loop(1, nyc, lambda t, number=number: pick_copy(number, t).wait_send())

    def drain(t):
        tell(t).wait_send()
        one(t).wait_send()

    loop(1, nyc, drain)
    loop(1, nz, lambda t: two(t).wait_send())
    loop(1, group, lambda t: three(t).wait_send())


def body(ny, nx, a_blocks, a_nbrs, p_blocks, p_dest, p_far_agg, agg_id, ap_slot, c_slot, send_rows):
    nz = NZ
    half = nz // 2
    nyc = ny * NC
    ml, tr = B // nyc, nyc * AGG
    sl, near_rows = ml * R, ml * AGG
    width = KC * B
    dma = pltpu.SemaphoreType.DMA
    block = lambda *lead: pltpu.VMEM(lead + (B, 128), bf16)
    smem = pl.BlockSpec(memory_space=pltpu.SMEM)
    scratch = [block(R) for _ in range(nz - 1)] + [
        pltpu.VMEM((R, B, KA * B), bf16),
        pltpu.VMEM((nz, 8, 128), i32),
        pltpu.VMEM((nz, 8, 128), i32),
        pltpu.SMEM((nz, 8, 128), i32),
        pltpu.SMEM((R * KA,), i32),
        block(nyc, nz * 2),
        block(R + nyc * nz * 2),
        pltpu.VMEM((3, B * R, 128), f32),
        pltpu.VMEM((AGG, B, width), f32),
        pltpu.VMEM((nyc, sl + near_rows, width), bf16),
        pltpu.VMEM((nyc, sl + near_rows, width), bf16),
        pltpu.VMEM((8, 128), i32),
        pltpu.VMEM((nyc, 8, 128), i32),
        pltpu.VMEM((nz, ml * tr, width), bf16),
        pltpu.VMEM((nz, ml * tr, width), bf16),
        pltpu.VMEM((3, ml * tr, 128), f32),
        pltpu.VMEM((nyc, near_rows, width), bf16),
        pltpu.VMEM((nx * nyc, near_rows, width), bf16),
        dma,
        dma((2, half, R // CHUNK)), dma((2, half, R // CHUNK)),
        dma((nz,)), dma((nz,)), dma,
        dma((half + 1, nyc)), dma((half + 1, nyc)),
        dma((nyc,)), dma((nyc,)), dma((nyc,)), dma((nyc,)),
        dma((nz,)), dma((nz,)),
        dma((nx * nyc,)), dma((nx * nyc,)),
    ]
    return pl.pallas_call(
        functools.partial(kernel, ny, nx),
        out_shape=jax.ShapeDtypeStruct((nx * AGG, B, width), bf16),
        in_specs=[smem] * 7 + [pl.BlockSpec(memory_space=pl.ANY), pl.BlockSpec(memory_space=pltpu.VMEM)],
        out_specs=pl.BlockSpec(memory_space=pltpu.VMEM),
        scratch_shapes=scratch,
        compiler_params=pltpu.CompilerParams(collective_id=0, has_side_effects=True, vmem_limit_bytes=40 * 2**20),
    )(a_nbrs, p_dest, p_far_agg, agg_id, ap_slot, c_slot, send_rows, a_blocks, p_blocks)


def solution(mesh):
    ny = mesh.shape["dom"] // (NZ * NC)
    nx = mesh.shape["sub"]
    both = ("dom", "sub")
    return jax.shard_map(
        functools.partial(body, ny, nx),
        mesh=mesh,
        in_specs=(
            P(both, None, None),
            P(both, None),
            P(both, None, None),
            P(both, None),
            P(both, None),
            P(both, None),
            P(both, None, None),
            P(both, None, None),
            P(both, None),
        ),
        out_specs=P("dom", None, None),
        check_vma=False,
    )
```

```python
import functools

import jax
import jax.numpy as jnp
from jax import lax
from jax.experimental import pallas as pl
from jax.experimental.pallas import tpu as pltpu
from jax.sharding import PartitionSpec as P

MESH = pl.DeviceIdType.MESH
NZ = 8
NC = 2
R = 16
KA = 7
B = 64
AGG = 2
KC = 6
CHUNK = 8
EARLY = 1
WINDOW = 3
f32, bf16, i32 = jnp.float32, jnp.bfloat16, jnp.int32

UNROLL = 4
PARTS = 2


def div(value, size):
    return value >> (size.bit_length() - 1)


def mod(value, size):
    return value & (size - 1)


def kernel(ny, nx, *refs):
    nz, nc = NZ, NC
    half = nz // 2
    nyc = ny * nc
    ml = B // nyc
    tr = nyc * AGG
    mc = ml // PARTS
    sl = mc * R
    near_rows = ml * AGG
    ints, (a_hbm, p_hbm, out_ref), scr = refs[:7], refs[7:10], list(refs[10:])
    int_s = [scr.pop(0) for _ in ints]
    nbr_s, dest_s, far_s, agg_s, slot_s, cslot_s, send_s = int_s
    p_ref, p_sem, int_sem = scr.pop(0), scr.pop(0), scr.pop(0)
    zr = [scr.pop(0) for _ in range(half - 1)]
    zl = [scr.pop(0) for _ in range(half - 1)]
    (zfar, a_vm, idx_out, idx_in, idx_s, cols_s, picks, ext, pt, ap_vm, wbuf, near, wsend, r1, near_in, meta_out, meta_in, dense, two_out, two_in, total, osend, r3,
     a_sem, s_ring, r_ring, s_idx, r_idx, l_idx, s_pick, r_pick, s_one, r_one, s_near, r_near, s_meta, r_meta, s_two, r_two, s_three, r_three) = scr

    dom, x = lax.axis_index("dom"), lax.axis_index("sub")
    y = div(dom, nz * nc)
    z = mod(div(dom, nc), nz)
    c = mod(dom, nc)
    j = y * nc + c
    turn = 1 - 2 * c

    def along_z(step):
        return ((y * nz + mod(z + step + nz, nz)) * nc + c, x)

    def in_plane(peer, px):
        return ((div(peer, nc) * nz + z) * nc + mod(peer, nc), px)

    def remote(src, dst, send, recv, device):
        return pltpu.make_async_remote_copy(
            src_ref=src, dst_ref=dst, send_sem=send, recv_sem=recv, device_id=device, device_id_type=MESH
        )

    def loop(lo, hi, fn):
        lax.fori_loop(lo, hi, lambda t, carry: (fn(t), carry)[1], 0)

    barrier = pltpu.get_barrier_semaphore()
    group = nx * nyc
    place = x * nyc + j
    int_copies = [pltpu.make_async_copy(src, dst, int_sem.at[n]) for n, (src, dst) in enumerate(zip(ints, int_s))]
    for copy in int_copies[::-1]:
        copy.start()
    p_copy = pltpu.make_async_copy(p_hbm, p_ref, p_sem)
    p_copy.start()
    loop(1, nz, lambda t: pl.semaphore_signal(barrier, inc=1, device_id=along_z(t), device_id_type=MESH))

    def greet(t):
        q = mod(place + t, group)
        pl.semaphore_signal(barrier, inc=1, device_id=in_plane(mod(q, nyc), div(q, nyc)), device_id_type=MESH)

    loop(1, group, greet)
    a_copy = pltpu.make_async_copy(a_hbm, a_vm, a_sem)
    a_copy.start()
    p_copy.wait()
    pl.semaphore_wait(barrier, nz - 1 + group - 1)

    def ring(way, step, piece):
        there = (zr, zl)[way]
        src = p_ref if step == 1 else there[step - 2]
        dst = there[step - 1] if step < half else zfar
        rows = pl.ds(piece * CHUNK, CHUNK)
        return remote(
            src.at[rows], dst.at[rows], s_ring.at[way, step - 1, piece], r_ring.at[way, step - 1, piece],
            along_z(turn if way == 0 else -turn),
        )

    pieces = R // CHUNK

    def order(way, step):
        listed = list(range(pieces)) if way == 0 else list(range(pieces))[::-1]
        return listed if step < half else listed[: pieces // 2]

    blocks = [(way, step) for step in range(1, half + 1) for way in (0, 1)]
    plan = [(way, step, piece) for way, step in blocks for piece in order(way, step)]
    begun = []

    def begin():
        if len(begun) >= WINDOW:
            ring(*plan[len(begun) - WINDOW]).wait_send()
        begun.append(plan[len(begun)])
        ring(*begun[-1]).start()

    for n in range(EARLY):
        begin()

    for copy in int_copies:
        copy.wait()

    lane = lax.broadcasted_iota(i32, (8, 128), 1)

    def list_for(t):
        zt = mod(z + turn * t + nz, nz)
        tile = jnp.zeros((8, 128), i32)
        for peer in range(nyc):
            for f in range(2):
                row = send_s[f, ((peer // nc) * nz + zt) * nc + peer % nc]
                tile = jnp.where(lane == peer * 2 + f, row, tile)
        return tile

    def slot_of(t):
        return 0 if t == 0 else 2 * t - 1 if t < half else nz - 1 if t == half else 2 * (nz - t)

    idx_in[0] = list_for(0)
    for t in range(1, nz):
        idx_out[t] = list_for(t)

    index_copies = [
        remote(idx_out.at[t], idx_in.at[slot_of(t)], s_idx.at[t], r_idx.at[t], along_z(turn * t)) for t in range(1, nz)
    ]
    for copy in index_copies:
        copy.start()
    while len(begun) < WINDOW:
        begin()

    def pick_copy(slot, t):
        return remote(
            picks.at[t, pl.ds(slot * 2, 2)], ext.at[pl.ds(R + (j * nz + slot) * 2, 2)],
            s_pick.at[slot, t], r_pick.at[slot, t], in_plane(mod(j + t, nyc), x),
        )

    def pick(slot, source, index):
        for f in range(2):
            ext[R + (j * nz + slot) * 2 + f] = source[index(j, f)]

        def for_peer(t):
            peer = mod(j + t, nyc)
            for f in range(2):
                picks[t, slot * 2 + f] = source[index(peer, f)]
            pick_copy(slot, t).start()

        loop(1, nyc, for_peer)

    pick(0, p_ref, lambda peer, f: send_s[f, (div(peer, nc) * nz + z) * nc + mod(peer, nc)])
    def place_row(i):
        cols_s[i * KA] = i
        for k in range(1, KA):
            n = nbr_s[k - 1, i]
            e = n - R
            f = e & 1
            owner = e >> 1
            oc = owner & (nc - 1)
            oz = (owner >> (nc.bit_length() - 1)) & (nz - 1)
            oy = owner >> ((nz * nc).bit_length() - 1)
            dz = (jnp.where(oc == 0, oz - z, z - oz) + nz) & (nz - 1)
            slot = jnp.where(dz == half, nz - 1, jnp.where(dz < half, 2 * dz, 2 * (nz - dz) - 1))
            cols_s[i * KA + k] = jnp.where(n < R, n, R + ((oy * nc + oc) * nz + slot) * 2 + f)

    def pick_block(way, step):
        if (way, step) == (0, 1):
            for copy in index_copies:
                copy.wait()
            to_scalars = pltpu.make_async_copy(idx_in, idx_s, l_idx)
            to_scalars.start()
            to_scalars.wait()
        slot = 2 * step - 1 + way if step < half else nz - 1
        pick(slot, (zr, zl)[way][step - 1] if step < half else zfar, lambda peer, f: idx_s[slot, 0, peer * 2 + f])

    line = lax.broadcasted_iota(i32, (2 * B, 128), 0)
    part, share_of, rest = div(line, nyc * mc), mod(div(line, mc), nyc), mod(line, mc)
    source = jnp.where(line < B, B + share_of * ml + part * mc + rest, line - B)
    reorder = jnp.where(lax.broadcasted_iota(i32, (2 * B, 128), 1) == source, 1.0, 0.0).astype(bf16)

    def transpose(i):
        pt[i] = lax.dot_general(reorder, p_ref[i], (((1,), (1,)), ((), ())), preferred_element_type=f32).astype(bf16)

    for way, step in blocks:
        listed = order(way, step)
        for piece in listed:
            if step > 1:
                ring(way, step - 1, piece).wait_recv()
                if piece == listed[-1]:
                    for other in order(way, step - 1):
                        if other not in listed:
                            ring(way, step - 1, other).wait_recv()
                    pick_block(way, step - 1)
            if (way, step, piece) not in plan[:WINDOW]:
                begin()
    for way in (0, 1):
        for piece in order(way, half):
            ring(way, half, piece).wait_recv()
    pick_block(0, half)
    loop(0, R, place_row)
    ext[0:R] = p_ref[...]
    lax.fori_loop(0, R, lambda t, carry: (transpose(t), carry)[1], 0, unroll=4)
    for slot in range(nz):
        loop(1, nyc, lambda t, slot=slot: pick_copy(slot, t).wait_recv())
    a_copy.wait()

    lane1 = lax.broadcasted_iota(i32, (1, 128), 1)
    low = lane1 < B
    high = jnp.where(low, 0, 1)
    low_mask = jnp.where(low, 1.0, 0.0).astype(bf16)
    high_mask = jnp.where(low, 0.0, 1.0).astype(bf16)
    near[...] = jnp.zeros_like(near)

    def masks(s0, s1, pairs):
        same = jnp.where(low, s0, s1) - high
        cross = jnp.where(low, s1, s0) - high
        return [
            (jnp.where(same == 2 * q, 1.0, 0.0).astype(f32), jnp.where(cross == 2 * q, 1.0, 0.0).astype(f32))
            for q in range(pairs)
        ]

    def row(i):
        ap = [None] * 4

        def merge(k, q):
            turned = pltpu.roll(q, B, 1)
            for n, (same, cross) in enumerate(masks(slot_s[k, 0, i], slot_s[k, 1, i], 4)):
                term = q * same + turned * cross
                ap[n] = term if ap[n] is None else ap[n] + term

        for pair in range(KA // 2):
            a = a_vm[i, :, pair * 128:(pair + 1) * 128]
            left = jnp.concatenate([a * low_mask, a * high_mask], axis=0)
            right = jnp.concatenate([ext[cols_s[i * KA + 2 * pair]], ext[cols_s[i * KA + 2 * pair + 1]]], axis=0)
            q = jnp.dot(left, right, preferred_element_type=f32)
            merge(2 * pair, q[:B])
            merge(2 * pair + 1, q[B:])
        q = jnp.dot(a_vm[i, :, (KA - 1) * B:], ext[cols_s[i * KA + KA - 1]], preferred_element_type=f32)
        merge(KA - 1, q)
        ap_vm[i] = jnp.concatenate([block.astype(bf16) for block in ap], axis=1)

    def rows(fn):
        lax.fori_loop(0, R, lambda t, carry: (fn(t), carry)[1], 0, unroll=UNROLL)

    rows(row)

    def coarse_row(i, m, lines):
        w = jnp.dot(lines, ap_vm[i], preferred_element_type=f32)
        to = [None] * 3
        for q in range(4):
            block = w[:, q * 128:(q + 1) * 128]
            turned = pltpu.roll(block, B, 1)
            for n, (same, cross) in enumerate(masks(cslot_s[m, 2 * q, i], cslot_s[m, 2 * q + 1, i], 3)):
                term = block * same + turned * cross
                to[n] = term if to[n] is None else to[n] + term
        return to

    meta = jnp.zeros((8, 128), i32)
    for i in range(R):
        d = dest_s[0, i]
        dc = d & (nc - 1)
        dz = (d >> (nc.bit_length() - 1)) & (nz - 1)
        dy = d >> ((nz * nc).bit_length() - 1)
        meta = jnp.where(lane == j * R + i, dz * tr + (dy * nc + dc) * AGG + far_s[0, i], meta)
    meta_out[...] = meta

    def share(part, peer):
        for n in range(3):
            wsend[part, peer, :, n * 128:(n + 1) * 128] = wbuf[part, n, pl.ds(peer * sl, sl), :].astype(bf16)

    def one(part, t):
        peer = mod(j + t, nyc)
        return remote(wsend.at[part, peer], r1.at[part, j], s_one.at[part, t], r_one.at[part, t], in_plane(peer, x))

    def tell(t):
        return remote(meta_out, meta_in.at[j], s_meta.at[t], r_meta.at[t], in_plane(mod(j + t, nyc), x))

    def send_near(t):
        return remote(near, near_in.at[x], s_near.at[t], r_near.at[t], (dom, mod(x + t, nx)))

    loop(1, nyc, lambda t: tell(t).start())
    meta_in[j] = meta_out[...]
    for part in range(PARTS):
        def far_row(i, part=part):
            for n, lines in enumerate(coarse_row(i, 1, pt[i, part * nyc * mc:(part + 1) * nyc * mc, :])):
                wbuf[part, n, pl.ds(i, nyc * mc, stride=R), :] = lines

        rows(far_row)

        def send_one(t, part=part):
            share(part, mod(j + t, nyc))
            one(part, t).start()

        loop(1, nyc, send_one)
        share(part, j)
        r1[part, j] = wsend[part, j]

    def near_row(i):
        agg = agg_s[0, i]
        for n, lines in enumerate(coarse_row(i, 0, pt[i, B:2 * B, :])):
            for g in range(AGG):
                near[g, :, n * 128:(n + 1) * 128] += lines * jnp.where(agg == g, 1.0, 0.0).astype(f32)

    rows(near_row)

    loop(1, nx, lambda t: send_near(t).start())
    near_in[x] = near[...]

    loop(1, nyc, lambda t: tell(t).wait_recv())
    told = meta_in[0]
    for peer in range(1, nyc):
        told = told + meta_in[peer]
    width = nyc * R
    aimed = lax.broadcasted_iota(i32, (nz * tr, width), 0) == told[0:1, 0:width]
    aimed = jnp.where(aimed, 1.0, 0.0).astype(bf16)

    deep = mc * tr
    cut = deep // 2

    def two(part, way, step):
        rows = pl.ds(way * cut, cut) if step == 1 else pl.ds(0, deep)
        return remote(
            two_out.at[part, way, step - 1, rows], two_in.at[part, way, step - 1, rows],
            s_two.at[part, way, step - 1], r_two.at[part, way, step - 1], along_z(1 - 2 * way),
        )

    def pass_on(part, step):
        for way in (0, 1):
            own = dense.at[part, mod(z + (1 - 2 * way) * (half - step + 1) + nz, nz)]
            out = two_out.at[part, way, step - 1]
            if step > 1:
                two(part, way, step - 1).wait_recv()
            for first in (0, cut):
                rows = slice(first, first + cut)
                if step == 1 and first != way * cut:
                    continue
                value = own[rows]
                if step > 2 or (step == 2 and first == way * cut):
                    value = value + two_in[part, way, step - 2, rows].astype(f32)
                out[rows] = value.astype(bf16)
            two(part, way, step).start()

    def finish(part):
        sums = dense[part, z]
        for way in (0, 1):
            two(part, way, half).wait_recv()
            sums = sums + two_in[part, way, half - 1].astype(f32)
        for n in range(3):
            total[n, part * deep:(part + 1) * deep, :] = sums[:, n * 128:(n + 1) * 128]

    for turn_of in range(PARTS + half):
        if turn_of < PARTS:
            part = turn_of
            loop(1, nyc, lambda t, part=part: one(part, t).wait_recv())
            for m in range(mc):
                lines = jnp.concatenate([r1[part, peer, m * R:(m + 1) * R, :] for peer in range(nyc)], axis=0)
                summed = jnp.dot(aimed, lines, preferred_element_type=f32)
                for zt in range(nz):
                    dense[part, zt, m * tr:(m + 1) * tr, :] = summed[zt * tr:(zt + 1) * tr]
        for part in range(max(0, turn_of - half), min(PARTS, turn_of + 1)):
            step = turn_of - part + 1
            if step <= half:
                pass_on(part, step)
            else:
                finish(part)

    for peer in range(nyc):
        lines = [
            jnp.concatenate([total[n, pl.ds(peer * AGG + g, ml, stride=tr), :] for g in range(AGG)], axis=0)
            for n in range(3)
        ]
        osend[peer] = jnp.concatenate(lines, axis=1).astype(bf16)

    def three(t):
        q = mod(place + t, group)
        peer = mod(q, nyc)
        return remote(osend.at[peer], r3.at[place], s_three.at[t], r_three.at[t], in_plane(peer, div(q, nyc)))

    loop(1, group, lambda t: three(t).start())
    r3[place] = osend[j]
    loop(1, nx, lambda t: send_near(t).wait_recv())
    loop(1, group, lambda t: three(t).wait_recv())
    for px in range(nx):
        for g in range(AGG):
            lines = [r3[px * nyc + peer].astype(f32)[g * ml:(g + 1) * ml] for peer in range(nyc)]
            out_ref[px * AGG + g] = (jnp.concatenate(lines, axis=0) + near_in[px, g]).astype(bf16)

    for item in plan[len(plan) - WINDOW:]:
        ring(*item).wait_send()
    for slot in range(nz):
        loop(1, nyc, lambda t, slot=slot: pick_copy(slot, t).wait_send())

    def drain(t):
        tell(t).wait_send()
        for part in range(PARTS):
            one(part, t).wait_send()

    loop(1, nyc, drain)
    loop(1, nx, lambda t: send_near(t).wait_send())
    for part in range(PARTS):
        for way in (0, 1):
            for step in range(1, half + 1):
                two(part, way, step).wait_send()
    loop(1, group, lambda t: three(t).wait_send())


def body(ny, nx, a_blocks, a_nbrs, p_blocks, p_dest, p_far_agg, agg_id, ap_slot, c_slot, send_rows):
    nz = NZ
    half = nz // 2
    nyc = ny * NC
    ml, tr = B // nyc, nyc * AGG
    mc = ml // PARTS
    sl, near_rows = mc * R, ml * AGG
    width = KC * B
    dma = pltpu.SemaphoreType.DMA
    block = lambda *lead: pltpu.VMEM(lead + (B, 128), bf16)
    ints = (a_nbrs.T, p_dest.T, p_far_agg.T, agg_id, ap_slot.transpose(1, 2, 0), c_slot.transpose(1, 2, 0), send_rows.T)
    scratch = [pltpu.SMEM(array.shape, i32) for array in ints] + [block(R), dma, dma((len(ints),))]
    scratch += [block(R) for _ in range(nz - 1)] + [
        pltpu.VMEM((R, B, KA * B), bf16),
        pltpu.VMEM((nz, 8, 128), i32),
        pltpu.VMEM((nz, 8, 128), i32),
        pltpu.SMEM((nz, 8, 128), i32),
        pltpu.SMEM((R * KA,), i32),
        block(nyc, nz * 2),
        block(R + nyc * nz * 2),
        pltpu.VMEM((R, 2 * B, B), bf16),
        pltpu.VMEM((R, B, 4 * 128), bf16),
        pltpu.VMEM((PARTS, 3, nyc * sl, 128), f32),
        pltpu.VMEM((AGG, B, width), f32),
        pltpu.VMEM((PARTS, nyc, sl, width), bf16),
        pltpu.VMEM((PARTS, nyc, sl, width), bf16),
        pltpu.VMEM((nx, AGG, B, width), f32),
        pltpu.VMEM((8, 128), i32),
        pltpu.VMEM((nyc, 8, 128), i32),
        pltpu.VMEM((PARTS, nz, mc * tr, width), f32),
        pltpu.VMEM((PARTS, 2, half, mc * tr, width), bf16),
        pltpu.VMEM((PARTS, 2, half, mc * tr, width), bf16),
        pltpu.VMEM((3, ml * tr, 128), f32),
        pltpu.VMEM((nyc, near_rows, width), bf16),
        pltpu.VMEM((nx * nyc, near_rows, width), bf16),
        dma,
        dma((2, half, R // CHUNK)), dma((2, half, R // CHUNK)),
        dma((nz,)), dma((nz,)), dma,
        dma((nz, nyc)), dma((nz, nyc)),
        dma((PARTS, nyc)), dma((PARTS, nyc)), dma((nyc,)), dma((nyc,)), dma((nyc,)), dma((nyc,)),
        dma((PARTS, 2, half)), dma((PARTS, 2, half)),
        dma((nx * nyc,)), dma((nx * nyc,)),
    ]
    return pl.pallas_call(
        functools.partial(kernel, ny, nx),
        out_shape=jax.ShapeDtypeStruct((nx * AGG, B, width), bf16),
        in_specs=[pl.BlockSpec(memory_space=pl.ANY)] * (len(ints) + 2),
        out_specs=pl.BlockSpec(memory_space=pltpu.VMEM),
        scratch_shapes=scratch,
        compiler_params=pltpu.CompilerParams(collective_id=0, has_side_effects=True, vmem_limit_bytes=62 * 2**20),
    )(*ints, a_blocks, p_blocks)


def solution(mesh):
    ny = mesh.shape["dom"] // (NZ * NC)
    nx = mesh.shape["sub"]
    both = ("dom", "sub")
    return jax.shard_map(
        functools.partial(body, ny, nx),
        mesh=mesh,
        in_specs=(
            P(both, None, None),
            P(both, None),
            P(both, None, None),
            P(both, None),
            P(both, None),
            P(both, None),
            P(both, None, None),
            P(both, None, None),
            P(both, None),
        ),
        out_specs=P("dom", None, None),
        check_vma=False,
    )
```

```python
import functools

import jax
import jax.numpy as jnp
from jax import lax
from jax.experimental import pallas as pl
from jax.experimental.pallas import tpu as pltpu
from jax.sharding import PartitionSpec as P

MESH = pl.DeviceIdType.MESH
NZ = 8
NC = 2
R = 16
KA = 7
B = 64
AGG = 2
KC = 6
CHUNK = 8
EARLY = 1
f32, bf16, i32 = jnp.float32, jnp.bfloat16, jnp.int32

UNROLL = 8
PARTS = 2


def div(value, size):
    return value >> (size.bit_length() - 1)


def mod(value, size):
    return value & (size - 1)


def kernel(ny, nx, *refs):
    nz, nc = NZ, NC
    half = nz // 2
    nyc = ny * nc
    ml = B // nyc
    tr = nyc * AGG
    mc = ml // PARTS
    sl = mc * R
    near_rows = ml * AGG
    ints, (a_hbm, p_hbm, out_ref), scr = refs[:7], refs[7:10], list(refs[10:])
    int_s = [scr.pop(0) for _ in ints]
    nbr_s, dest_s, far_s, agg_s, slot_s, cslot_s, send_s = int_s
    p_ref, p_sem, int_sem = scr.pop(0), scr.pop(0), scr.pop(0)
    zr = [scr.pop(0) for _ in range(half - 1)]
    zl = [scr.pop(0) for _ in range(half - 1)]
    (zfar, a_vm, idx_out, idx_in, idx_s, cols_s, picks, ext, pt, ap_vm, wbuf, near, wsend, r1, near_in, meta_out, meta_in, dense, two_out, two_in, total, osend, r3,
     a_sem, s_ring, r_ring, s_idx, r_idx, l_idx, s_pick, r_pick, s_one, r_one, s_near, r_near, s_meta, r_meta, s_two, r_two, s_three, r_three) = scr

    dom, x = lax.axis_index("dom"), lax.axis_index("sub")
    y = div(dom, nz * nc)
    z = mod(div(dom, nc), nz)
    c = mod(dom, nc)
    j = y * nc + c
    turn = 1 - 2 * c

    def along_z(step):
        return ((y * nz + mod(z + step + nz, nz)) * nc + c, x)

    def in_plane(peer, px):
        return ((div(peer, nc) * nz + z) * nc + mod(peer, nc), px)

    def remote(src, dst, send, recv, device):
        return pltpu.make_async_remote_copy(
            src_ref=src, dst_ref=dst, send_sem=send, recv_sem=recv, device_id=device, device_id_type=MESH
        )

    def loop(lo, hi, fn):
        lax.fori_loop(lo, hi, lambda t, carry: (fn(t), carry)[1], 0)

    barrier = pltpu.get_barrier_semaphore()
    group = nx * nyc
    place = x * nyc + j
    int_copies = [pltpu.make_async_copy(src, dst, int_sem.at[n]) for n, (src, dst) in enumerate(zip(ints, int_s))]
    for copy in int_copies[::-1]:
        copy.start()
    p_copy = pltpu.make_async_copy(p_hbm, p_ref, p_sem)
    p_copy.start()
    loop(1, nz, lambda t: pl.semaphore_signal(barrier, inc=1, device_id=along_z(t), device_id_type=MESH))

    def greet(t):
        q = mod(place + t, group)
        pl.semaphore_signal(barrier, inc=1, device_id=in_plane(mod(q, nyc), div(q, nyc)), device_id_type=MESH)

    loop(1, group, greet)
    a_copy = pltpu.make_async_copy(a_hbm, a_vm, a_sem)
    a_copy.start()
    p_copy.wait()
    pl.semaphore_wait(barrier, nz - 1 + group - 1)

    def ring(way, step, piece):
        there = (zr, zl)[way]
        src = p_ref if step == 1 else there[step - 2]
        dst = there[step - 1] if step < half else zfar
        rows = pl.ds(piece * CHUNK, CHUNK)
        return remote(
            src.at[rows], dst.at[rows], s_ring.at[way, step - 1, piece], r_ring.at[way, step - 1, piece],
            along_z(turn if way == 0 else -turn),
        )

    pieces = R // CHUNK

    def order(way, step):
        listed = list(range(pieces)) if way == 0 else list(range(pieces))[::-1]
        return listed if step < half else listed[: pieces // 2]

    blocks = [(way, step) for step in range(1, half + 1) for way in (0, 1)]
    plan = [(way, step, piece) for way, step in blocks for piece in order(way, step)]
    begun = []

    def begin():
        begun.append(plan[len(begun)])
        ring(*begun[-1]).start()

    for n in range(EARLY):
        begin()

    for copy in int_copies:
        copy.wait()

    lane = lax.broadcasted_iota(i32, (8, 128), 1)

    def list_for(t):
        zt = mod(z + turn * t + nz, nz)
        tile = jnp.zeros((8, 128), i32)
        for peer in range(nyc):
            for f in range(2):
                row = send_s[f, ((peer // nc) * nz + zt) * nc + peer % nc]
                tile = jnp.where(lane == peer * 2 + f, row, tile)
        return tile

    def slot_of(t):
        return 0 if t == 0 else 2 * t - 1 if t < half else nz - 1 if t == half else 2 * (nz - t)

    idx_in[0] = list_for(0)
    for t in range(1, nz):
        idx_out[t] = list_for(t)

    index_copies = [
        remote(idx_out.at[t], idx_in.at[slot_of(t)], s_idx.at[t], r_idx.at[t], along_z(turn * t)) for t in range(1, nz)
    ]
    for copy in index_copies:
        copy.start()
    while len(begun) < 2 * pieces:
        begin()

    def pick_copy(slot, t):
        return remote(
            picks.at[t, pl.ds(slot * 2, 2)], ext.at[pl.ds(R + (j * nz + slot) * 2, 2)],
            s_pick.at[slot, t], r_pick.at[slot, t], in_plane(mod(j + t, nyc), x),
        )

    def pick(slot, source, index):
        for f in range(2):
            ext[R + (j * nz + slot) * 2 + f] = source[index(j, f)]

        def for_peer(t):
            peer = mod(j + t, nyc)
            for f in range(2):
                picks[t, slot * 2 + f] = source[index(peer, f)]
            pick_copy(slot, t).start()

        loop(1, nyc, for_peer)

    pick(0, p_ref, lambda peer, f: send_s[f, (div(peer, nc) * nz + z) * nc + mod(peer, nc)])
    def place_row(i):
        cols_s[i * KA] = i
        for k in range(1, KA):
            n = nbr_s[k - 1, i]
            e = n - R
            f = e & 1
            owner = e >> 1
            oc = owner & (nc - 1)
            oz = (owner >> (nc.bit_length() - 1)) & (nz - 1)
            oy = owner >> ((nz * nc).bit_length() - 1)
            dz = (jnp.where(oc == 0, oz - z, z - oz) + nz) & (nz - 1)
            slot = jnp.where(dz == half, nz - 1, jnp.where(dz < half, 2 * dz, 2 * (nz - dz) - 1))
            cols_s[i * KA + k] = jnp.where(n < R, n, R + ((oy * nc + oc) * nz + slot) * 2 + f)

    def pick_block(way, step):
        if (way, step) == (0, 1):
            for copy in index_copies:
                copy.wait()
            to_scalars = pltpu.make_async_copy(idx_in, idx_s, l_idx)
            to_scalars.start()
            to_scalars.wait()
        slot = 2 * step - 1 + way if step < half else nz - 1
        pick(slot, (zr, zl)[way][step - 1] if step < half else zfar, lambda peer, f: idx_s[slot, 0, peer * 2 + f])

    line = lax.broadcasted_iota(i32, (2 * B, 128), 0)
    part, share_of, rest = div(line, nyc * mc), mod(div(line, mc), nyc), mod(line, mc)
    source = jnp.where(line < B, B + share_of * ml + part * mc + rest, line - B)
    reorder = jnp.where(lax.broadcasted_iota(i32, (2 * B, 128), 1) == source, 1.0, 0.0).astype(bf16)

    def transpose(i):
        pt[i] = lax.dot_general(reorder, p_ref[i], (((1,), (1,)), ((), ())), preferred_element_type=f32).astype(bf16)

    for way, step in blocks:
        listed = order(way, step)
        for piece in listed:
            if step > 1:
                ring(way, step - 1, piece).wait_recv()
                if piece == listed[-1]:
                    for other in order(way, step - 1):
                        if other not in listed:
                            ring(way, step - 1, other).wait_recv()
                    pick_block(way, step - 1)
                begin()
    for way in (0, 1):
        for piece in order(way, half):
            ring(way, half, piece).wait_recv()
    pick_block(0, half)
    meta = jnp.zeros((8, 128), i32)
    for i in range(R):
        d = dest_s[0, i]
        dc = d & (nc - 1)
        dz = (d >> (nc.bit_length() - 1)) & (nz - 1)
        dy = d >> ((nz * nc).bit_length() - 1)
        meta = jnp.where(lane == j * R + i, dz * tr + (dy * nc + dc) * AGG + far_s[0, i], meta)
    meta_out[...] = meta

    def tell(t):
        return remote(meta_out, meta_in.at[j], s_meta.at[t], r_meta.at[t], in_plane(mod(j + t, nyc), x))

    loop(1, nyc, lambda t: tell(t).start())
    meta_in[j] = meta_out[...]
    loop(0, R, place_row)
    ext[0:R] = p_ref[...]
    lax.fori_loop(0, R, lambda t, carry: (transpose(t), carry)[1], 0, unroll=4)
    for slot in range(nz):
        loop(1, nyc, lambda t, slot=slot: pick_copy(slot, t).wait_recv())
    a_copy.wait()

    lane1 = lax.broadcasted_iota(i32, (1, 128), 1)
    low = lane1 < B
    high = jnp.where(low, 0, 1)
    low_mask = jnp.where(low, 1.0, 0.0).astype(bf16)
    high_mask = jnp.where(low, 0.0, 1.0).astype(bf16)
    near[...] = jnp.zeros_like(near)

    def masks(s0, s1, pairs):
        same = jnp.where(low, s0, s1) - high
        cross = jnp.where(low, s1, s0) - high
        return [
            (jnp.where(same == 2 * q, 1.0, 0.0).astype(f32), jnp.where(cross == 2 * q, 1.0, 0.0).astype(f32))
            for q in range(pairs)
        ]

    def row(i):
        ap = [None] * 4

        def merge(k, q):
            turned = pltpu.roll(q, B, 1)
            for n, (same, cross) in enumerate(masks(slot_s[k, 0, i], slot_s[k, 1, i], 4)):
                term = q * same + turned * cross
                ap[n] = term if ap[n] is None else ap[n] + term

        for pair in range(KA // 2):
            a = a_vm[i, :, pair * 128:(pair + 1) * 128]
            left = jnp.concatenate([a * low_mask, a * high_mask], axis=0)
            right = jnp.concatenate([ext[cols_s[i * KA + 2 * pair]], ext[cols_s[i * KA + 2 * pair + 1]]], axis=0)
            q = jnp.dot(left, right, preferred_element_type=f32)
            merge(2 * pair, q[:B])
            merge(2 * pair + 1, q[B:])
        q = jnp.dot(a_vm[i, :, (KA - 1) * B:], ext[cols_s[i * KA + KA - 1]], preferred_element_type=f32)
        merge(KA - 1, q)
        ap_vm[i] = jnp.concatenate([block.astype(bf16) for block in ap], axis=1)

    def rows(fn):
        lax.fori_loop(0, R, lambda t, carry: (fn(t), carry)[1], 0, unroll=UNROLL)

    def coarse_row(i, m, lines):
        w = jnp.dot(lines, ap_vm[i], preferred_element_type=f32)
        to = [None] * 3
        for q in range(4):
            block = w[:, q * 128:(q + 1) * 128]
            turned = pltpu.roll(block, B, 1)
            for n, (same, cross) in enumerate(masks(cslot_s[m, 2 * q, i], cslot_s[m, 2 * q + 1, i], 3)):
                term = block * same + turned * cross
                to[n] = term if to[n] is None else to[n] + term
        return to

    def share(part, peer):
        for n in range(3):
            wsend[part, peer, :, n * 128:(n + 1) * 128] = wbuf[part, n, pl.ds(peer * sl, sl), :].astype(bf16)

    def one(part, t):
        peer = mod(j + t, nyc)
        return remote(wsend.at[part, peer], r1.at[part, j], s_one.at[part, t], r_one.at[part, t], in_plane(peer, x))

    def send_near(t):
        return remote(near, near_in.at[x], s_near.at[t], r_near.at[t], (dom, mod(x + t, nx)))

    rows(row)
    for part in range(PARTS):
        def far_row(i, part=part):
            for n, lines in enumerate(coarse_row(i, 1, pt[i, part * nyc * mc:(part + 1) * nyc * mc, :])):
                wbuf[part, n, pl.ds(i, nyc * mc, stride=R), :] = lines

        rows(far_row)

        def send_one(t, part=part):
            share(part, mod(j + t, nyc))
            one(part, t).start()

        loop(1, nyc, send_one)
        share(part, j)
        r1[part, j] = wsend[part, j]

    def near_row(i):
        agg = agg_s[0, i]
        for n, lines in enumerate(coarse_row(i, 0, pt[i, B:2 * B, :])):
            for g in range(AGG):
                near[g, :, n * 128:(n + 1) * 128] += lines * jnp.where(agg == g, 1.0, 0.0).astype(f32)

    rows(near_row)

    loop(1, nx, lambda t: send_near(t).start())
    near_in[x] = near[...]

    loop(1, nyc, lambda t: tell(t).wait_recv())
    told = meta_in[0]
    for peer in range(1, nyc):
        told = told + meta_in[peer]
    width = nyc * R
    aimed = lax.broadcasted_iota(i32, (nz * tr, width), 0) == told[0:1, 0:width]
    aimed = jnp.where(aimed, 1.0, 0.0).astype(bf16)

    deep = mc * tr
    cut = deep // 2

    def two(part, way, step):
        rows = pl.ds(way * cut, cut) if step == 1 else pl.ds(0, deep)
        return remote(
            two_out.at[part, way, step - 1, rows], two_in.at[part, way, step - 1, rows],
            s_two.at[part, way, step - 1], r_two.at[part, way, step - 1], along_z(1 - 2 * way),
        )

    def pass_on(part, step):
        for way in (0, 1):
            own = dense.at[part, mod(z + (1 - 2 * way) * (half - step + 1) + nz, nz)]
            out = two_out.at[part, way, step - 1]
            if step > 1:
                two(part, way, step - 1).wait_recv()
            for first in (0, cut):
                rows = slice(first, first + cut)
                if step == 1 and first != way * cut:
                    continue
                value = own[rows]
                if step > 2 or (step == 2 and first == way * cut):
                    value = value + two_in[part, way, step - 2, rows].astype(f32)
                out[rows] = value.astype(bf16)
            two(part, way, step).start()

    def finish(part):
        sums = dense[part, z]
        for way in (0, 1):
            two(part, way, half).wait_recv()
            sums = sums + two_in[part, way, half - 1].astype(f32)
        for n in range(3):
            total[n, part * deep:(part + 1) * deep, :] = sums[:, n * 128:(n + 1) * 128]

    def merge_part(part):
        loop(1, nyc, lambda t: one(part, t).wait_recv())
        for m in range(mc):
            lines = jnp.concatenate([r1[part, peer, m * R:(m + 1) * R, :] for peer in range(nyc)], axis=0)
            summed = jnp.dot(aimed, lines, preferred_element_type=f32)
            for zt in range(nz):
                dense[part, zt, m * tr:(m + 1) * tr, :] = summed[zt * tr:(zt + 1) * tr]

    for step, part in [(step, part) for step in range(half + 2) for part in range(PARTS)]:
        if step == 0:
            merge_part(part)
        elif step <= half:
            pass_on(part, step)
        else:
            finish(part)

    for peer in range(nyc):
        lines = [
            jnp.concatenate([total[n, pl.ds(peer * AGG + g, ml, stride=tr), :] for g in range(AGG)], axis=0)
            for n in range(3)
        ]
        osend[peer] = jnp.concatenate(lines, axis=1).astype(bf16)

    def three(t):
        q = mod(place + t, group)
        peer = mod(q, nyc)
        return remote(osend.at[peer], r3.at[place], s_three.at[t], r_three.at[t], in_plane(peer, div(q, nyc)))

    loop(1, group, lambda t: three(t).start())
    r3[place] = osend[j]

    for item in plan:
        ring(*item).wait_send()
    for slot in range(nz):
        loop(1, nyc, lambda t, slot=slot: pick_copy(slot, t).wait_send())

    def drain(t):
        tell(t).wait_send()
        for part in range(PARTS):
            one(part, t).wait_send()

    loop(1, nyc, drain)
    loop(1, nx, lambda t: send_near(t).wait_send())
    for part in range(PARTS):
        for way in (0, 1):
            for step in range(1, half + 1):
                two(part, way, step).wait_send()
    loop(1, group, lambda t: three(t).wait_send())

    loop(1, nx, lambda t: send_near(t).wait_recv())
    loop(1, group, lambda t: three(t).wait_recv())
    for px in range(nx):
        for g in range(AGG):
            lines = [r3[px * nyc + peer].astype(f32)[g * ml:(g + 1) * ml] for peer in range(nyc)]
            out_ref[px * AGG + g] = (jnp.concatenate(lines, axis=0) + near_in[px, g]).astype(bf16)


def body(ny, nx, a_blocks, a_nbrs, p_blocks, p_dest, p_far_agg, agg_id, ap_slot, c_slot, send_rows):
    nz = NZ
    half = nz // 2
    nyc = ny * NC
    ml, tr = B // nyc, nyc * AGG
    mc = ml // PARTS
    sl, near_rows = mc * R, ml * AGG
    width = KC * B
    dma = pltpu.SemaphoreType.DMA
    block = lambda *lead: pltpu.VMEM(lead + (B, 128), bf16)
    ints = (a_nbrs.T, p_dest.T, p_far_agg.T, agg_id, ap_slot.transpose(1, 2, 0), c_slot.transpose(1, 2, 0), send_rows.T)
    scratch = [pltpu.SMEM(array.shape, i32) for array in ints] + [block(R), dma, dma((len(ints),))]
    scratch += [block(R) for _ in range(nz - 1)] + [
        pltpu.VMEM((R, B, KA * B), bf16),
        pltpu.VMEM((nz, 8, 128), i32),
        pltpu.VMEM((nz, 8, 128), i32),
        pltpu.SMEM((nz, 8, 128), i32),
        pltpu.SMEM((R * KA,), i32),
        block(nyc, nz * 2),
        block(R + nyc * nz * 2),
        pltpu.VMEM((R, 2 * B, B), bf16),
        pltpu.VMEM((R, B, 4 * 128), bf16),
        pltpu.VMEM((PARTS, 3, nyc * sl, 128), f32),
        pltpu.VMEM((AGG, B, width), f32),
        pltpu.VMEM((PARTS, nyc, sl, width), bf16),
        pltpu.VMEM((PARTS, nyc, sl, width), bf16),
        pltpu.VMEM((nx, AGG, B, width), f32),
        pltpu.VMEM((8, 128), i32),
        pltpu.VMEM((nyc, 8, 128), i32),
        pltpu.VMEM((PARTS, nz, mc * tr, width), f32),
        pltpu.VMEM((PARTS, 2, half, mc * tr, width), bf16),
        pltpu.VMEM((PARTS, 2, half, mc * tr, width), bf16),
        pltpu.VMEM((3, ml * tr, 128), f32),
        pltpu.VMEM((nyc, near_rows, width), bf16),
        pltpu.VMEM((nx * nyc, near_rows, width), bf16),
        dma,
        dma((2, half, R // CHUNK)), dma((2, half, R // CHUNK)),
        dma((nz,)), dma((nz,)), dma,
        dma((nz, nyc)), dma((nz, nyc)),
        dma((PARTS, nyc)), dma((PARTS, nyc)), dma((nyc,)), dma((nyc,)), dma((nyc,)), dma((nyc,)),
        dma((PARTS, 2, half)), dma((PARTS, 2, half)),
        dma((nx * nyc,)), dma((nx * nyc,)),
    ]
    return pl.pallas_call(
        functools.partial(kernel, ny, nx),
        out_shape=jax.ShapeDtypeStruct((nx * AGG, B, width), bf16),
        in_specs=[pl.BlockSpec(memory_space=pl.ANY)] * (len(ints) + 2),
        out_specs=pl.BlockSpec(memory_space=pltpu.VMEM),
        scratch_shapes=scratch,
        compiler_params=pltpu.CompilerParams(collective_id=0, has_side_effects=True, vmem_limit_bytes=62 * 2**20),
    )(*ints, a_blocks, p_blocks)


def solution(mesh):
    ny = mesh.shape["dom"] // (NZ * NC)
    nx = mesh.shape["sub"]
    both = ("dom", "sub")
    return jax.shard_map(
        functools.partial(body, ny, nx),
        mesh=mesh,
        in_specs=(
            P(both, None, None),
            P(both, None),
            P(both, None, None),
            P(both, None),
            P(both, None),
            P(both, None),
            P(both, None, None),
            P(both, None, None),
            P(both, None),
        ),
        out_specs=P("dom", None, None),
        check_vma=False,
    )
```

```python
import functools

import jax
import jax.numpy as jnp
from jax import lax
from jax.experimental import pallas as pl
from jax.experimental.pallas import tpu as pltpu
from jax.sharding import PartitionSpec as P

MESH = pl.DeviceIdType.MESH
NZ = 8
NC = 2
R = 16
KA = 7
B = 64
AGG = 2
KC = 6
CHUNK = 8
EARLY = 1
f32, bf16, i32 = jnp.float32, jnp.bfloat16, jnp.int32

UNROLL = 8
PARTS = 2


def div(value, size):
    return value >> (size.bit_length() - 1)


def mod(value, size):
    return value & (size - 1)


def kernel(ny, nx, *refs):
    nz, nc = NZ, NC
    half = nz // 2
    nyc = ny * nc
    ml = B // nyc
    tr = nyc * AGG
    mc = ml // PARTS
    sl = mc * R
    near_rows = ml * AGG
    ints, (a_hbm, p_hbm, out_ref), scr = refs[:7], refs[7:10], list(refs[10:])
    int_s = [scr.pop(0) for _ in ints]
    nbr_s, dest_s, far_s, agg_s, slot_s, cslot_s, send_s = int_s
    p_ref, p_sem, int_sem = scr.pop(0), scr.pop(0), scr.pop(0)
    zr = [scr.pop(0) for _ in range(half - 1)]
    zl = [scr.pop(0) for _ in range(half - 1)]
    (zfar, a_vm, idx_out, idx_in, idx_s, cols_s, picks, ext, pt, ap_vm, wbuf, near, wsend, r1, near_in, meta_out, meta_in, dense, two_out, two_in, total, osend, r3,
     a_sem, s_ring, r_ring, s_idx, r_idx, l_idx, s_pick, r_pick, s_one, r_one, s_near, r_near, s_meta, r_meta, s_two, r_two, s_three, r_three) = scr

    dom, x = lax.axis_index("dom"), lax.axis_index("sub")
    y = div(dom, nz * nc)
    z = mod(div(dom, nc), nz)
    c = mod(dom, nc)
    j = y * nc + c
    turn = 1 - 2 * c

    def along_z(step):
        return ((y * nz + mod(z + step + nz, nz)) * nc + c, x)

    def in_plane(peer, px):
        return ((div(peer, nc) * nz + z) * nc + mod(peer, nc), px)

    def remote(src, dst, send, recv, device):
        return pltpu.make_async_remote_copy(
            src_ref=src, dst_ref=dst, send_sem=send, recv_sem=recv, device_id=device, device_id_type=MESH
        )

    def loop(lo, hi, fn):
        lax.fori_loop(lo, hi, lambda t, carry: (fn(t), carry)[1], 0)

    barrier = pltpu.get_barrier_semaphore()
    group = nx * nyc
    place = x * nyc + j
    int_copies = [pltpu.make_async_copy(src, dst, int_sem.at[n]) for n, (src, dst) in enumerate(zip(ints, int_s))]
    for copy in int_copies[::-1]:
        copy.start()
    p_copy = pltpu.make_async_copy(p_hbm, p_ref, p_sem)
    p_copy.start()
    loop(1, nz, lambda t: pl.semaphore_signal(barrier, inc=1, device_id=along_z(t), device_id_type=MESH))

    def greet(t):
        q = mod(place + t, group)
        pl.semaphore_signal(barrier, inc=1, device_id=in_plane(mod(q, nyc), div(q, nyc)), device_id_type=MESH)

    loop(1, group, greet)
    a_copy = pltpu.make_async_copy(a_hbm, a_vm, a_sem)
    a_copy.start()
    p_copy.wait()
    pl.semaphore_wait(barrier, nz - 1 + group - 1)

    def ring(way, step, piece):
        there = (zr, zl)[way]
        src = p_ref if step == 1 else there[step - 2]
        dst = there[step - 1] if step < half else zfar
        rows = pl.ds(piece * CHUNK, CHUNK)
        return remote(
            src.at[rows], dst.at[rows], s_ring.at[way, step - 1, piece], r_ring.at[way, step - 1, piece],
            along_z(turn if way == 0 else -turn),
        )

    pieces = R // CHUNK

    def order(way, step):
        listed = list(range(pieces)) if way == 0 else list(range(pieces))[::-1]
        return listed if step < half else listed[: pieces // 2]

    blocks = [(way, step) for step in range(1, half + 1) for way in (0, 1)]
    plan = [(way, step, piece) for way, step in blocks for piece in order(way, step)]
    begun = []

    def begin():
        begun.append(plan[len(begun)])
        ring(*begun[-1]).start()

    for n in range(EARLY):
        begin()

    for copy in int_copies:
        copy.wait()

    lane = lax.broadcasted_iota(i32, (8, 128), 1)

    def list_for(t):
        zt = mod(z + turn * t + nz, nz)
        tile = jnp.zeros((8, 128), i32)
        for peer in range(nyc):
            for f in range(2):
                row = send_s[f, ((peer // nc) * nz + zt) * nc + peer % nc]
                tile = jnp.where(lane == peer * 2 + f, row, tile)
        return tile

    def slot_of(t):
        return 0 if t == 0 else 2 * t - 1 if t < half else nz - 1 if t == half else 2 * (nz - t)

    idx_in[0] = list_for(0)
    for t in range(1, nz):
        idx_out[t] = list_for(t)

    index_copies = [
        remote(idx_out.at[t], idx_in.at[slot_of(t)], s_idx.at[t], r_idx.at[t], along_z(turn * t)) for t in range(1, nz)
    ]
    for copy in index_copies:
        copy.start()
    while len(begun) < 2 * pieces:
        begin()

    def pick_copy(slot, t):
        return remote(
            picks.at[t, pl.ds(slot * 2, 2)], ext.at[pl.ds(R + (j * nz + slot) * 2, 2)],
            s_pick.at[slot, t], r_pick.at[slot, t], in_plane(mod(j + t, nyc), x),
        )

    def pick(slot, source, index):
        for f in range(2):
            ext[R + (j * nz + slot) * 2 + f] = source[index(j, f)]

        def for_peer(t):
            peer = mod(j + t, nyc)
            for f in range(2):
                picks[t, slot * 2 + f] = source[index(peer, f)]
            pick_copy(slot, t).start()

        loop(1, nyc, for_peer)

    pick(0, p_ref, lambda peer, f: send_s[f, (div(peer, nc) * nz + z) * nc + mod(peer, nc)])
    def place_row(i):
        cols_s[i * KA] = i
        for k in range(1, KA):
            n = nbr_s[k - 1, i]
            e = n - R
            f = e & 1
            owner = e >> 1
            oc = owner & (nc - 1)
            oz = (owner >> (nc.bit_length() - 1)) & (nz - 1)
            oy = owner >> ((nz * nc).bit_length() - 1)
            dz = (jnp.where(oc == 0, oz - z, z - oz) + nz) & (nz - 1)
            slot = jnp.where(dz == half, nz - 1, jnp.where(dz < half, 2 * dz, 2 * (nz - dz) - 1))
            cols_s[i * KA + k] = jnp.where(n < R, n, R + ((oy * nc + oc) * nz + slot) * 2 + f)

    def pick_block(way, step):
        if (way, step) == (0, 1):
            for copy in index_copies:
                copy.wait()
            to_scalars = pltpu.make_async_copy(idx_in, idx_s, l_idx)
            to_scalars.start()
            to_scalars.wait()
        slot = 2 * step - 1 + way if step < half else nz - 1
        pick(slot, (zr, zl)[way][step - 1] if step < half else zfar, lambda peer, f: idx_s[slot, 0, peer * 2 + f])

    line = lax.broadcasted_iota(i32, (2 * B, 128), 0)
    part, share_of, rest = div(line, nyc * mc), mod(div(line, mc), nyc), mod(line, mc)
    source = jnp.where(line < B, B + share_of * ml + part * mc + rest, line - B)
    reorder = jnp.where(lax.broadcasted_iota(i32, (2 * B, 128), 1) == source, 1.0, 0.0).astype(bf16)

    def transpose(i):
        pt[i] = lax.dot_general(reorder, p_ref[i], (((1,), (1,)), ((), ())), preferred_element_type=f32).astype(bf16)

    for way, step in blocks:
        listed = order(way, step)
        for piece in listed:
            if step > 1:
                ring(way, step - 1, piece).wait_recv()
                if piece == listed[-1]:
                    for other in order(way, step - 1):
                        if other not in listed:
                            ring(way, step - 1, other).wait_recv()
                    pick_block(way, step - 1)
                begin()
    for way in (0, 1):
        for piece in order(way, half):
            ring(way, half, piece).wait_recv()
    pick_block(0, half)
    meta = jnp.zeros((8, 128), i32)
    for i in range(R):
        d = dest_s[0, i]
        dc = d & (nc - 1)
        dz = (d >> (nc.bit_length() - 1)) & (nz - 1)
        dy = d >> ((nz * nc).bit_length() - 1)
        meta = jnp.where(lane == j * R + i, dz * tr + (dy * nc + dc) * AGG + far_s[0, i], meta)
    meta_out[...] = meta

    def tell(t):
        return remote(meta_out, meta_in.at[j], s_meta.at[t], r_meta.at[t], in_plane(mod(j + t, nyc), x))

    loop(1, nyc, lambda t: tell(t).start())
    meta_in[j] = meta_out[...]
    loop(0, R, place_row)
    ext[0:R] = p_ref[...]
    lax.fori_loop(0, R, lambda t, carry: (transpose(t), carry)[1], 0, unroll=4)
    for slot in range(nz):
        loop(1, nyc, lambda t, slot=slot: pick_copy(slot, t).wait_recv())
    a_copy.wait()

    lane1 = lax.broadcasted_iota(i32, (1, 128), 1)
    low = lane1 < B
    high = jnp.where(low, 0, 1)
    low_mask = jnp.where(low, 1.0, 0.0).astype(bf16)
    high_mask = jnp.where(low, 0.0, 1.0).astype(bf16)
    near[...] = jnp.zeros_like(near)

    def masks(s0, s1, pairs):
        same = jnp.where(low, s0, s1) - high
        cross = jnp.where(low, s1, s0) - high
        return [
            (jnp.where(same == 2 * q, 1.0, 0.0).astype(f32), jnp.where(cross == 2 * q, 1.0, 0.0).astype(f32))
            for q in range(pairs)
        ]

    def row(i):
        def placed(k):
            block = ext[cols_s[i * KA + k]]
            turned = jnp.concatenate([block[:, B:], block[:, :B]], axis=1)
            pairs = masks(slot_s[k, 0, i], slot_s[k, 1, i], 4)
            return (
                jnp.concatenate([block * same.astype(bf16) for same, _ in pairs], axis=1),
                jnp.concatenate([turned * cross.astype(bf16) for _, cross in pairs], axis=1),
            )

        left, right = [], []
        for pair in range(KA // 2):
            first, second = placed(2 * pair), placed(2 * pair + 1)
            left += [a_vm[i, :, pair * 128:(pair + 1) * 128]] * 2
            right += [first[0], second[0], first[1], second[1]]
        ap = jnp.dot(jnp.concatenate(left, axis=1), jnp.concatenate(right, axis=0), preferred_element_type=f32)
        last = a_vm[i, :, (KA - 1) * B:]
        for block in placed(KA - 1):
            ap = ap + jnp.dot(last, block, preferred_element_type=f32)
        ap_vm[i] = ap.astype(bf16)

    def rows(fn):
        lax.fori_loop(0, R, lambda t, carry: (fn(t), carry)[1], 0, unroll=UNROLL)

    def coarse_row(i, m, lines):
        w = jnp.dot(lines, ap_vm[i], preferred_element_type=f32)
        to = [None] * 3
        for q in range(4):
            block = w[:, q * 128:(q + 1) * 128]
            turned = pltpu.roll(block, B, 1)
            for n, (same, cross) in enumerate(masks(cslot_s[m, 2 * q, i], cslot_s[m, 2 * q + 1, i], 3)):
                term = block * same + turned * cross
                to[n] = term if to[n] is None else to[n] + term
        return to

    def share(part, peer):
        for n in range(3):
            wsend[part, peer, :, n * 128:(n + 1) * 128] = wbuf[part, n, pl.ds(peer * sl, sl), :].astype(bf16)

    def one(part, t):
        peer = mod(j + t, nyc)
        return remote(wsend.at[part, peer], r1.at[part, j], s_one.at[part, t], r_one.at[part, t], in_plane(peer, x))

    def send_near(t):
        return remote(near, near_in.at[x], s_near.at[t], r_near.at[t], (dom, mod(x + t, nx)))

    rows(row)
    for part in range(PARTS):
        def far_row(i, part=part):
            for n, lines in enumerate(coarse_row(i, 1, pt[i, part * nyc * mc:(part + 1) * nyc * mc, :])):
                wbuf[part, n, pl.ds(i, nyc * mc, stride=R), :] = lines

        rows(far_row)

        def send_one(t, part=part):
            share(part, mod(j + t, nyc))
            one(part, t).start()

        loop(1, nyc, send_one)
        share(part, j)
        r1[part, j] = wsend[part, j]

    def near_row(i):
        agg = agg_s[0, i]
        for n, lines in enumerate(coarse_row(i, 0, pt[i, B:2 * B, :])):
            for g in range(AGG):
                near[g, :, n * 128:(n + 1) * 128] += lines * jnp.where(agg == g, 1.0, 0.0).astype(f32)

    rows(near_row)

    loop(1, nx, lambda t: send_near(t).start())
    near_in[x] = near[...]

    loop(1, nyc, lambda t: tell(t).wait_recv())
    told = meta_in[0]
    for peer in range(1, nyc):
        told = told + meta_in[peer]
    width = nyc * R
    aimed = lax.broadcasted_iota(i32, (nz * tr, width), 0) == told[0:1, 0:width]
    aimed = jnp.where(aimed, 1.0, 0.0).astype(bf16)

    deep = mc * tr
    cut = deep // 2

    def two(part, way, step):
        rows = pl.ds(way * cut, cut) if step == 1 else pl.ds(0, deep)
        return remote(
            two_out.at[part, way, step - 1, rows], two_in.at[part, way, step - 1, rows],
            s_two.at[part, way, step - 1], r_two.at[part, way, step - 1], along_z(1 - 2 * way),
        )

    def pass_on(part, step):
        for way in (0, 1):
            own = dense.at[part, mod(z + (1 - 2 * way) * (half - step + 1) + nz, nz)]
            out = two_out.at[part, way, step - 1]
            if step > 1:
                two(part, way, step - 1).wait_recv()
            for first in (0, cut):
                rows = slice(first, first + cut)
                if step == 1 and first != way * cut:
                    continue
                value = own[rows]
                if step > 2 or (step == 2 and first == way * cut):
                    value = value + two_in[part, way, step - 2, rows].astype(f32)
                out[rows] = value.astype(bf16)
            two(part, way, step).start()

    def finish(part):
        sums = dense[part, z]
        for way in (0, 1):
            two(part, way, half).wait_recv()
            sums = sums + two_in[part, way, half - 1].astype(f32)
        for n in range(3):
            total[n, part * deep:(part + 1) * deep, :] = sums[:, n * 128:(n + 1) * 128]

    def merge_part(part):
        loop(1, nyc, lambda t: one(part, t).wait_recv())
        for m in range(mc):
            lines = jnp.concatenate([r1[part, peer, m * R:(m + 1) * R, :] for peer in range(nyc)], axis=0)
            summed = jnp.dot(aimed, lines, preferred_element_type=f32)
            for zt in range(nz):
                dense[part, zt, m * tr:(m + 1) * tr, :] = summed[zt * tr:(zt + 1) * tr]

    for step, part in [(step, part) for step in range(half + 2) for part in range(PARTS)]:
        if step == 0:
            merge_part(part)
        elif step <= half:
            pass_on(part, step)
        else:
            finish(part)

    for peer in range(nyc):
        lines = [
            jnp.concatenate([total[n, pl.ds(peer * AGG + g, ml, stride=tr), :] for g in range(AGG)], axis=0)
            for n in range(3)
        ]
        osend[peer] = jnp.concatenate(lines, axis=1).astype(bf16)

    def three(t):
        q = mod(place + t, group)
        peer = mod(q, nyc)
        return remote(osend.at[peer], r3.at[place], s_three.at[t], r_three.at[t], in_plane(peer, div(q, nyc)))

    loop(1, group, lambda t: three(t).start())
    r3[place] = osend[j]

    for item in plan:
        ring(*item).wait_send()
    for slot in range(nz):
        loop(1, nyc, lambda t, slot=slot: pick_copy(slot, t).wait_send())

    def drain(t):
        tell(t).wait_send()
        for part in range(PARTS):
            one(part, t).wait_send()

    loop(1, nyc, drain)
    loop(1, nx, lambda t: send_near(t).wait_send())
    for part in range(PARTS):
        for way in (0, 1):
            for step in range(1, half + 1):
                two(part, way, step).wait_send()
    loop(1, group, lambda t: three(t).wait_send())

    loop(1, nx, lambda t: send_near(t).wait_recv())
    loop(1, group, lambda t: three(t).wait_recv())
    for px in range(nx):
        for g in range(AGG):
            lines = [r3[px * nyc + peer].astype(f32)[g * ml:(g + 1) * ml] for peer in range(nyc)]
            out_ref[px * AGG + g] = (jnp.concatenate(lines, axis=0) + near_in[px, g]).astype(bf16)


def body(ny, nx, a_blocks, a_nbrs, p_blocks, p_dest, p_far_agg, agg_id, ap_slot, c_slot, send_rows):
    nz = NZ
    half = nz // 2
    nyc = ny * NC
    ml, tr = B // nyc, nyc * AGG
    mc = ml // PARTS
    sl, near_rows = mc * R, ml * AGG
    width = KC * B
    dma = pltpu.SemaphoreType.DMA
    block = lambda *lead: pltpu.VMEM(lead + (B, 128), bf16)
    ints = (a_nbrs.T, p_dest.T, p_far_agg.T, agg_id, ap_slot.transpose(1, 2, 0), c_slot.transpose(1, 2, 0), send_rows.T)
    scratch = [pltpu.SMEM(array.shape, i32) for array in ints] + [block(R), dma, dma((len(ints),))]
    scratch += [block(R) for _ in range(nz - 1)] + [
        pltpu.VMEM((R, B, KA * B), bf16),
        pltpu.VMEM((nz, 8, 128), i32),
        pltpu.VMEM((nz, 8, 128), i32),
        pltpu.SMEM((nz, 8, 128), i32),
        pltpu.SMEM((R * KA,), i32),
        block(nyc, nz * 2),
        block(R + nyc * nz * 2),
        pltpu.VMEM((R, 2 * B, B), bf16),
        pltpu.VMEM((R, B, 4 * 128), bf16),
        pltpu.VMEM((PARTS, 3, nyc * sl, 128), f32),
        pltpu.VMEM((AGG, B, width), f32),
        pltpu.VMEM((PARTS, nyc, sl, width), bf16),
        pltpu.VMEM((PARTS, nyc, sl, width), bf16),
        pltpu.VMEM((nx, AGG, B, width), f32),
        pltpu.VMEM((8, 128), i32),
        pltpu.VMEM((nyc, 8, 128), i32),
        pltpu.VMEM((PARTS, nz, mc * tr, width), f32),
        pltpu.VMEM((PARTS, 2, half, mc * tr, width), bf16),
        pltpu.VMEM((PARTS, 2, half, mc * tr, width), bf16),
        pltpu.VMEM((3, ml * tr, 128), f32),
        pltpu.VMEM((nyc, near_rows, width), bf16),
        pltpu.VMEM((nx * nyc, near_rows, width), bf16),
        dma,
        dma((2, half, R // CHUNK)), dma((2, half, R // CHUNK)),
        dma((nz,)), dma((nz,)), dma,
        dma((nz, nyc)), dma((nz, nyc)),
        dma((PARTS, nyc)), dma((PARTS, nyc)), dma((nyc,)), dma((nyc,)), dma((nyc,)), dma((nyc,)),
        dma((PARTS, 2, half)), dma((PARTS, 2, half)),
        dma((nx * nyc,)), dma((nx * nyc,)),
    ]
    return pl.pallas_call(
        functools.partial(kernel, ny, nx),
        out_shape=jax.ShapeDtypeStruct((nx * AGG, B, width), bf16),
        in_specs=[pl.BlockSpec(memory_space=pl.ANY)] * (len(ints) + 2),
        out_specs=pl.BlockSpec(memory_space=pltpu.VMEM),
        scratch_shapes=scratch,
        compiler_params=pltpu.CompilerParams(collective_id=0, has_side_effects=True, vmem_limit_bytes=62 * 2**20),
    )(*ints, a_blocks, p_blocks)


def solution(mesh):
    ny = mesh.shape["dom"] // (NZ * NC)
    nx = mesh.shape["sub"]
    both = ("dom", "sub")
    return jax.shard_map(
        functools.partial(body, ny, nx),
        mesh=mesh,
        in_specs=(
            P(both, None, None),
            P(both, None),
            P(both, None, None),
            P(both, None),
            P(both, None),
            P(both, None),
            P(both, None, None),
            P(both, None, None),
            P(both, None),
        ),
        out_specs=P("dom", None, None),
        check_vma=False,
    )
```
